512 devices in a mesh: member: 8 (over z), lat: 16 (over x_lo, y), lon: 4 (over x_hi, core).
Axes of the slice: x: 4 (x_hi: 2, x_lo: 2; x = x_hi * 2 + x_lo), y: 8, z: 8, core: 2. Of those that a mesh axis runs over, the one named last changes fastest.
Arguments:
- inputs: bfloat16 [8, 512, 128, 512], P('member', None, 'lat', 'lon'), may hold values from -6 to 6
- weight: bfloat16 [3, 3, 100, 512], replicated, may hold values from -0.09375 to 0.09375
- bias: float32 [100], replicated, may hold values from -3 to 3
- observed: bfloat16 [100, 128, 512], P(None, 'lat', 'lon'), may hold values from -7 to 7
- channel_weight: float32 [100], replicated, may hold values from 1 to 8
Outputs:
- grad_input: bfloat16 [8, 512, 128, 512], P('member', None, 'lat', 'lon')
- grad_weight: bfloat16 [3, 3, 100, 512], replicated
- grad_bias: float32 [100], replicated
- score: bfloat16 [100, 128, 512], P(None, 'lat', 'lon')
The draws below stay inside these ranges and needn't reach their ends.
All inputs are finite; a program needn't handle non-finite values.
Results may differ from the reference program's by a relative error of at most 0.0023.
The reference program's roundings to bfloat16 on the way count: a program that leaves them out, or rounds other values in their place, can miss the bound.
Values may be sent and summed in bfloat16 or wider, within the bound.
A program may use at most 64 MiB of HBM per device.

```python
import math
import jax
import jax.numpy as jnp
from jax import lax

C_IN = 512
C_OUT = 100
MEMBERS = 8
LAT_ROWS = 128
LON_COLS = 512


def steps_of(key, extent, cuts, least, top_value):
    loudness = 1.0
    for position, shards_of in cuts:
        draws = jax.random.uniform(jax.random.fold_in(jax.random.fold_in(key, 6), position), (shards_of,), jnp.float32, least / len(cuts), top_value / len(cuts))
        loudness = loudness * jnp.repeat(jnp.exp(draws), extent[position] // shards_of).reshape((-1,) + (1,) * (len(extent) - 1 - position))
    return loudness


def normal_values(key, extent, spread, most, cuts=(), kind=jnp.bfloat16):
    factor_of = steps_of(key, extent, cuts, -0.22, 0.18) if cuts else 1.0
    entries = jax.random.normal(key, extent, jnp.float32) * spread * factor_of
    return jnp.minimum(jnp.maximum(entries, -most), most).astype(kind)


def setup_inputs(seed: int = 0) -> dict:
    key_list = jax.random.split(jax.random.key(seed), 6)
    return {
        "inputs": normal_values(key_list[0], (MEMBERS, C_IN, LAT_ROWS, LON_COLS), 1.0, 6.0, ((0, 8), (2, 16), (3, 4))),
        "weight": normal_values(key_list[1], (3, 3, C_OUT, C_IN), (9 * C_IN) ** -0.5, 0.09375),
        "bias": normal_values(key_list[2], (C_OUT,), 0.5, 3.0, (), jnp.float32),
        "observed": normal_values(key_list[3], (C_OUT, LAT_ROWS, LON_COLS), 1.2, 7.0, ((1, 16), (2, 4))),
        "channel_weight": jnp.clip(jnp.exp(jax.random.uniform(key_list[4], (C_OUT,), jnp.float32, math.log(1.0), math.log(8.0))), 1.0, 8.0),
    }


smooth_width = 0.25

def pad_field(field):
    rows = jnp.pad(field, ((0, 0), (1, 1), (0, 0)))
    return jnp.concatenate([rows[:, :, -1:], rows, rows[:, :, :1]], axis=2)

def forward_member(member_input, weight, bias):
    padded = pad_field(member_input).astype(jnp.float32)
    kernel = weight.astype(jnp.float32)
    total = jnp.zeros((C_OUT, LAT_ROWS, LON_COLS), jnp.float32) + bias[:, None, None]
    for i in range(3):
        for j in range(3):
            total = total + jnp.einsum('oc,chw->ohw', kernel[i, j], padded[:, i:i + LAT_ROWS, j:j + LON_COLS], precision=lax.Precision.HIGHEST)
    return total.astype(jnp.bfloat16)

def backward_member(grad_field, weight):
    padded = pad_field(grad_field).astype(jnp.float32)
    kernel = weight.astype(jnp.float32)
    total = jnp.zeros((C_IN, LAT_ROWS, LON_COLS), jnp.float32)
    for i in range(3):
        for j in range(3):
            total = total + jnp.einsum('oc,ohw->chw', kernel[i, j], padded[:, 2 - i:2 - i + LAT_ROWS, 2 - j:2 - j + LON_COLS], precision=lax.Precision.HIGHEST)
    return total.astype(jnp.bfloat16)

def reference(inputs, weight, bias, observed, channel_weight):
    fields = lax.map(lambda one: forward_member(one, weight, bias), inputs)
    obs = observed.astype(jnp.float32)
    rows = jnp.arange(LAT_ROWS).astype(jnp.float32)
    area = jnp.cos(math.pi * (rows + 0.5) / LAT_ROWS - math.pi / 2)
    scale = channel_weight[:, None, None] * (area / jnp.mean(area))[None, :, None]

    def one_member(carry, field):
        own = field.astype(jnp.float32)

        def add_other(inner, other):
            diff = own - other.astype(jnp.float32)
            root = jnp.sqrt(diff * diff + smooth_width * smooth_width)
            return ((inner[0] + root, inner[1] + diff / root), None)
        zero = jnp.zeros_like(own)
        (pair, slope), _ = lax.scan(add_other, (zero, zero), fields)
        gap = own - obs
        gap_root = jnp.sqrt(gap * gap + smooth_width * smooth_width)
        grad = (scale * (gap / gap_root / MEMBERS - slope / (MEMBERS * (MEMBERS - 1)))).astype(jnp.bfloat16)
        return ((carry[0] + gap_root, carry[1] + pair), grad)
    start = jnp.zeros((C_OUT, LAT_ROWS, LON_COLS), jnp.float32)
    (gap_total, pair_total), grads = lax.scan(one_member, (start, start), fields)
    score = (gap_total / MEMBERS - pair_total / (2 * MEMBERS * (MEMBERS - 1))).astype(jnp.bfloat16)
    grad_input = lax.map(lambda g: backward_member(g, weight), grads)

    def add_kernel(carry, pair_in):
        member_input, grad_field = pair_in
        padded = pad_field(member_input).astype(jnp.float32)
        wide_grad = grad_field.astype(jnp.float32)
        pieces = []
        for i in range(3):
            for j in range(3):
                pieces.append(jnp.einsum('ohw,chw->oc', wide_grad, padded[:, i:i + LAT_ROWS, j:j + LON_COLS], precision=lax.Precision.HIGHEST))
        kernel = jnp.stack(pieces).reshape(3, 3, C_OUT, C_IN)
        return ((carry[0] + kernel, carry[1] + lax.optimization_barrier(jnp.sum(wide_grad, axis=(1, 2)))), None)
    init = (jnp.zeros((3, 3, C_OUT, C_IN), jnp.float32), jnp.zeros((C_OUT,), jnp.float32))
    (kernel_sum, bias_sum), _ = lax.scan(add_kernel, init, (inputs, grads))
    factor = 1.0 / math.sqrt(MEMBERS * LAT_ROWS * LON_COLS)
    return (grad_input, (kernel_sum * factor).astype(jnp.bfloat16), bias_sum * factor, score)
```

```python
import functools
import math

import jax
import jax.numpy as jnp
from jax import lax
from jax.experimental import pallas as pl
from jax.experimental.pallas import tpu as pltpu
from jax.sharding import PartitionSpec as P

smooth = 0.0625
MESH = pl.DeviceIdType.MESH
F32 = jnp.float32
BF16 = jnp.bfloat16
NN = (((1,), (0,)), ((), ()))
NT = (((1,), (1,)), ((), ()))
OP = 112
OF = 104


def mm(a, b, dims=NN):
    return lax.dot_general(a, b, dims, preferred_element_type=F32)


def rcopy(src, dst, ssem, rsem, dev):
    return pltpu.make_async_remote_copy(
        src_ref=src, dst_ref=dst, send_sem=ssem, recv_sem=rsem,
        device_id=dev, device_id_type=MESH,
    )


def kernel(
    sizes,
    x_ref, w_ref, bias_ref, obs_ref, cw_ref, area_ref,
    gi_ref, gw_ref, gb_ref, score_ref,
    xf, xs, ws, wt, y, hs, hr, rows_s, rows_r, fs, fr, of, gs, gr, sc_s, sc_r,
    ce_s, ce_r, rh, gt, d4, rc, rsum, r1, s2, r2, x3, t_b, g1, g2, gif,
    sem_h, sem_row, sem_f, sem_g, sem_sc, sem_rh, sem_ce,
    sem_core, sem_1, sem_2, sem_x, sem_g1, sem_g2, sem_gc,
):
    NM, NLAT, NLON, NY, NX = sizes
    C = x_ref.shape[0]
    CO = obs_ref.shape[0]
    R = x_ref.shape[1]
    m = lax.axis_index("member")
    a = lax.axis_index("lat")
    b = lax.axis_index("lon")
    xl, yy = a // NY, a % NY
    xh, core = b // 2, b % 2
    xx = xh * 2 + xl
    up = a > 0
    down = a < NLAT - 1
    left = lax.rem(b + NLON - 1, NLON)
    right = lax.rem(b + 1, NLON)
    a_up = jnp.maximum(a - 1, 0)
    a_dn = jnp.minimum(a + 1, NLAT - 1)

    def dev_z(p):
        return (p, a, b)

    def dev_y(p):
        return (m, xl * NY + p, b)

    def dev_x(p):
        return (m, (p % 2) * NY + yy, (p // 2) * 2 + core)

    other_core = (m, a, xh * 2 + 1 - core)

    def each(n, fn):
        def body(d, carry):
            fn(d)
            return carry
        lax.fori_loop(1, n, body, 0)

    bar = pltpu.get_barrier_semaphore()

    def greet(dev):
        pl.semaphore_signal(bar, inc=1, device_id=dev, device_id_type=MESH)

    each(NM, lambda d: greet(dev_z(lax.rem(m + d, NM))))
    each(NY, lambda d: greet(dev_y(lax.rem(yy + d, NY))))
    each(NX, lambda d: greet(dev_x(lax.rem(xx + d, NX))))
    for bb in (left, right):
        greet((m, a, bb))

    @pl.when(up)
    def _():
        for bb in (b, left, right):
            greet((m, a_up, bb))

    @pl.when(down)
    def _():
        for bb in (b, left, right):
            greet((m, a_dn, bb))
    greet(other_core)

    xf[...] = x_ref[...].reshape(C * R, 128).astype(F32)
    for r in range(R):
        xs[:, r * 128:(r + 1) * 128] = xf[pl.ds(r, C, stride=R), :].astype(BF16)
    zpad = jnp.zeros((OP - CO, C), F32)
    for t in range(9):
        tap = w_ref[t // 3, t % 3].astype(F32)
        ws[t * OP:(t + 1) * OP, :] = jnp.concatenate([tap, zpad], axis=0).astype(BF16)

    cell = lax.broadcasted_iota(jnp.int32, (32, R * 128), 1)
    line = lax.broadcasted_iota(jnp.int32, (32, R * 128), 0)
    want = jnp.where(line < 16, line * 128, (line - 16) * 128 + 127)
    pick = jnp.where((cell == want) & (line % 16 < R), 1.0, 0.0).astype(BF16)
    hs[...] = mm(pick, xs[...], NT).astype(BF16).reshape(2, 16, C)

    n_hello = (NM - 1) + (NY - 1) + (NX - 1) + 3
    pl.semaphore_wait(bar, n_hello + 3 * up.astype(jnp.int32) + 3 * down.astype(jnp.int32))

    h_first = rcopy(hs.at[0], hr.at[1], sem_h.at[0], sem_h.at[3], (m, a, left))
    h_last = rcopy(hs.at[1], hr.at[0], sem_h.at[1], sem_h.at[2], (m, a, right))
    h_first.start()
    h_last.start()

    def fwd(n, carry):
        at = pl.ds(pl.multiple_of(n * 256, 256), 256)
        y[:, at] = mm(ws[...], xs[:, at])
        return carry
    lax.fori_loop(0, R // 2, fwd, 0)
    bt = jnp.broadcast_to(bias_ref[...], (128, 128)).T
    ct = jnp.broadcast_to(cw_ref[...], (128, 128)).T
    h_first.wait_recv()
    h_last.wait_recv()
    yh = mm(ws[...], hr[...].reshape(32, C), NT)

    lane = lax.broadcasted_iota(jnp.int32, (OF, 128), 1)

    def tap_rows(t):
        return slice(t * OP, t * OP + OF)

    def out_row(r):
        parts = []
        cols = []
        for j in range(3):
            total = None
            col = None
            for i in range(3):
                src = r + i - 1
                if 0 <= src < R:
                    piece = y[tap_rows(i * 3 + j), src * 128:(src + 1) * 128]
                    total = piece if total is None else total + piece
                    if j != 1:
                        at = src if j == 0 else 16 + src
                        edge = yh[tap_rows(i * 3 + j), at:at + 1]
                        col = edge if col is None else col + edge
            parts.append(total)
            cols.append(col)
        low = jnp.where(lane == 0, cols[0], pltpu.roll(parts[0], 1, 1))
        high = jnp.where(lane == 127, cols[2], pltpu.roll(parts[2], 127, 1))
        return parts[1] + low + high

    rows_s[0] = out_row(-1)
    rows_s[1] = out_row(R)
    row_up = rcopy(rows_s.at[0], rows_r.at[1], sem_row.at[0], sem_row.at[3], (m, a_up, b))
    row_dn = rcopy(rows_s.at[1], rows_r.at[0], sem_row.at[1], sem_row.at[2], (m, a_dn, b))

    @pl.when(up)
    def _():
        row_up.start()

    @pl.when(down)
    def _():
        row_dn.start()

    rows_r_zero = jnp.zeros((OF, 128), F32)
    pad8 = jnp.zeros((OP - OF, 128), F32)

    def pad16(v):
        return jnp.concatenate([v, pad8], axis=0).astype(BF16)

    for r in range(1, R - 1):
        fs[r] = pad16(out_row(r) + bt[:OF])
    first = out_row(0) + bt[:OF]
    last = out_row(R - 1) + bt[:OF]

    @pl.when(up)
    def _():
        row_dn.wait_recv()

    @pl.when(jnp.logical_not(up))
    def _():
        rows_r[0] = rows_r_zero

    @pl.when(down)
    def _():
        row_up.wait_recv()

    @pl.when(jnp.logical_not(down))
    def _():
        rows_r[1] = rows_r_zero
    fs[0] = pad16(first + rows_r[0])
    fs[R - 1] = pad16(last + rows_r[1])

    def f_copy(d):
        p = lax.rem(m + d, NM)
        return rcopy(fs.at[p], fr.at[m], sem_f.at[0, d], sem_f.at[1, d], dev_z(p))
    each(NM, lambda d: f_copy(d).start())
    fr[m] = fs[m]
    of[...] = jnp.concatenate(
        [obs_ref[...].reshape(CO * R, 128).astype(F32), jnp.zeros(((OF - CO) * R, 128), F32)], axis=0)
    obs = of[pl.ds(m, OF, stride=R), :]
    scale = ct[:OF] * area_ref[pl.ds(a * R + m, 1), :]
    each(NM, lambda d: f_copy(d).wait_recv())

    own = [fr[k][:OF].astype(F32) for k in range(NM)]
    slope = [None] * NM
    pair = jnp.full((OF, 128), NM * 0.5 * math.sqrt(smooth), F32)
    gap_total = jnp.zeros((OF, 128), F32)
    for k in range(NM):
        for n in range(k + 1, NM):
            diff = own[k] - own[n]
            sq = diff * diff + smooth
            inv = lax.rsqrt(sq)
            pair = pair + sq * inv
            s = diff * inv
            slope[k] = s if slope[k] is None else slope[k] + s
            slope[n] = -s if slope[n] is None else slope[n] - s
    for k in range(NM):
        gap = own[k] - obs
        sq = gap * gap + smooth
        inv = lax.rsqrt(sq)
        gap_total = gap_total + sq * inv
        gs[k] = pad16(scale * (gap * inv * (1.0 / NM) - slope[k] * (1.0 / (NM * (NM - 1)))))
    sc_s[...] = pad16(gap_total * (1.0 / NM) - pair * (1.0 / (NM * (NM - 1))))

    def g_copy(d):
        p = lax.rem(m + d, NM)
        return rcopy(gs.at[p], gr.at[m], sem_g.at[0, d], sem_g.at[1, d], dev_z(p))

    def sc_copy(d):
        p = lax.rem(m + d, NM)
        return rcopy(sc_s, sc_r.at[m], sem_sc.at[0, d], sem_sc.at[1, d], dev_z(p))
    each(NM, lambda d: g_copy(d).start())
    each(NM, lambda d: sc_copy(d).start())
    gr[m] = gs[m]
    sc_r[m] = sc_s[...]
    wt[:, :9 * OP] = ws[...].astype(F32).T.astype(BF16)
    wt[:, 9 * OP:] = jnp.zeros((C, 1024 - 9 * OP), BF16)
    each(NM, lambda d: g_copy(d).wait_recv())

    g_up = rcopy(gr.at[0], rh.at[1], sem_rh.at[0], sem_rh.at[3], (m, a_up, b))
    g_dn = rcopy(gr.at[R - 1], rh.at[0], sem_rh.at[1], sem_rh.at[2], (m, a_dn, b))

    @pl.when(up)
    def _():
        g_up.start()

    @pl.when(down)
    def _():
        g_dn.start()
    edges = []
    lane8 = lax.broadcasted_iota(jnp.int32, (8, 128), 1)
    line8 = lax.broadcasted_iota(jnp.int32, (8, 128), 0)
    pick2 = jnp.where(((line8 == 0) & (lane8 == 0)) | ((line8 == 1) & (lane8 == 127)), 1.0, 0.0).astype(BF16)
    for r in range(R):
        edges.append(mm(pick2, gr[r], NT))
    fill = jnp.zeros((16 - R, OP), F32)
    for side in range(2):
        stack = jnp.concatenate([e[side:side + 1] for e in edges] + [fill], axis=0)
        ce_s[side] = jnp.concatenate([stack, jnp.zeros((16, 128 - OP), F32)], axis=1).astype(BF16)

    def c_copy(v, s):
        aa = (a_dn, a, a_up)[v]
        bb = right if s == 0 else left
        return rcopy(ce_s.at[1 - s], ce_r.at[v, s], sem_ce.at[0, v, s], sem_ce.at[1, v, s], (m, aa, bb))

    for s in range(2):
        c_copy(1, s).start()

    @pl.when(down)
    def _():
        for s in range(2):
            c_copy(0, s).start()

    @pl.when(up)
    def _():
        for s in range(2):
            c_copy(2, s).start()

    for s in range(2):
        c_copy(1, s).wait_recv()

    @pl.when(up)
    def _():
        g_dn.wait_recv()
        for s in range(2):
            c_copy(0, s).wait_recv()

    @pl.when(jnp.logical_not(up))
    def _():
        rh[0] = jnp.zeros((OP, 128), BF16)
        for s in range(2):
            ce_r[0, s] = jnp.zeros((16, 128), BF16)

    @pl.when(down)
    def _():
        g_up.wait_recv()
        for s in range(2):
            c_copy(2, s).wait_recv()

    @pl.when(jnp.logical_not(down))
    def _():
        rh[1] = jnp.zeros((OP, 128), BF16)
        for s in range(2):
            ce_r[2, s] = jnp.zeros((16, 128), BF16)

    colt = []
    for s in range(2):
        above = ce_r[0, s].astype(F32)[R - 1:R]
        here = ce_r[1, s].astype(F32)[:R]
        below = ce_r[2, s].astype(F32)[0:1]
        stack = jnp.concatenate([above, here, below, jnp.zeros((128 - R - 2, 128), F32)], axis=0)
        colt.append(stack.T)
    lane_p = lax.broadcasted_iota(jnp.int32, (OP, 128), 1)
    for q in range(R + 2):
        r = q - 1
        mid = rh[0] if r < 0 else rh[1] if r >= R else gr[r]
        wide = mid.astype(F32)
        to_right = jnp.where(lane_p == 127, colt[1][:OP, q:q + 1], pltpu.roll(wide, 127, 1)).astype(BF16)
        to_left = jnp.where(lane_p == 0, colt[0][:OP, q:q + 1], pltpu.roll(wide, 1, 1)).astype(BF16)
        for i in range(3):
            here = r - 1 + i
            if 0 <= here < R:
                for j, v in enumerate((to_right, mid, to_left)):
                    t = i * 3 + j
                    gt[t * OP:(t + 1) * OP, here * 128:(here + 1) * 128] = v
    gt[9 * OP:, :] = jnp.zeros((1024 - 9 * OP, R * 128), BF16)

    half = C // 2

    def wgrad(h):
        at = pl.ds(pl.multiple_of(h * half, half), half)
        part = mm(gt[:9 * OP, :], xs[at, :], NT)
        for q in range(2):
            d4[h * 2 + q, :9 * OP, :] = part[:, q * 128:(q + 1) * 128]

    center = mm(jnp.ones((16, R * 128), BF16), gt[4 * OP:5 * OP, :], NT)
    bias_rows = jnp.concatenate([center, jnp.zeros((16, 128 - OP), F32)], axis=1)
    for q in range(4):
        d4[q, 9 * OP:, :] = bias_rows if q == 0 else jnp.zeros((16, 128), F32)
    wgrad(1 - core)
    core_copy = rcopy(d4.at[pl.ds(2 * (1 - core), 2)], rc, sem_core.at[0], sem_core.at[1], other_core)
    core_copy.start()
    wgrad(core)
    core_copy.wait_recv()
    rsum[...] = d4[pl.ds(2 * core, 2)] + rc[...]

    n1 = (NY, NM)
    me1 = (yy, m)
    dev1 = (dev_y, dev_z)
    n2 = (NM, NY)
    me2 = (m, yy)
    dev2 = (dev_z, dev_y)

    def copy1(q, d):
        p = lax.rem(me1[q] + d, n1[q])
        return rcopy(rsum.at[q, pl.ds(pl.multiple_of(p * 128, 128), 128)], r1.at[q, d],
                     sem_1.at[0, q, d], sem_1.at[1, q, d], dev1[q](p))

    def start1(d):
        for q in range(2):
            copy1(q, d).start()
    each(NY, start1)

    def bwd(n, carry):
        at = pl.ds(pl.multiple_of(n * 256, 256), 256)
        part = mm(wt[...], gt[:, at])
        for q in range(2):
            gif[pl.ds(2 * n + q, C, stride=R), :] = part[:, q * 128:(q + 1) * 128]
        return carry
    lax.fori_loop(0, R // 2, bwd, 0)
    gi_ref[...] = gif[...].reshape(C, R, 128).astype(BF16)
    each(NM, lambda d: sc_copy(d).wait_recv())
    for r in range(R):
        of[pl.ds(r, OF, stride=R), :] = sc_r[r].astype(F32)[:OF]
    score_ref[...] = of[:CO * R, :].reshape(CO, R, 128).astype(BF16)

    for q in range(2):
        total = rsum[q, pl.ds(pl.multiple_of(me1[q] * 128, 128), 128), :]
        for d in range(1, n1[q]):
            copy1(q, d).wait_recv()
            total = total + r1[q, d]
        s2[q] = total

    def copy2(q, d):
        p = lax.rem(me2[q] + d, n2[q])
        return rcopy(s2.at[q, pl.ds(pl.multiple_of(p * 16, 16), 16)], r2.at[q, d],
                     sem_2.at[0, q, d], sem_2.at[1, q, d], dev2[q](p))

    def start2(d):
        for q in range(2):
            copy2(q, d).start()
    each(NY, start2)
    for q in range(2):
        total = s2[q, pl.ds(pl.multiple_of(me2[q] * 16, 16), 16), :]
        for d in range(1, n2[q]):
            copy2(q, d).wait_recv()
            total = total + r2[q, d]
        x3[xx, q] = total

    def copy3(d):
        p = lax.rem(xx + d, NX)
        return rcopy(x3.at[xx], x3.at[xx], sem_x.at[0, d], sem_x.at[1, d], dev_x(p))
    each(NX, lambda d: copy3(d).start())
    each(NX, lambda d: copy3(d).wait_recv())
    factor = 1.0 / math.sqrt(NM * NLAT * R * NLON * 128)
    sub = lax.broadcasted_iota(jnp.int32, (16, 128), 0)
    for q in range(2):
        total = x3[0, q]
        for p in range(1, NX):
            total = total + x3[p, q]
        total = total * factor
        high = total.astype(BF16).astype(F32)
        rest = total - high
        middle = rest.astype(BF16).astype(F32)
        low = rest - middle
        row = me1[q] * 128 + me2[q] * 16 + sub
        t_b[q] = jnp.where(row == 9 * OP + 1, middle, jnp.where(row == 9 * OP + 2, low, high)).astype(BF16)

    def copy_g1(q, d):
        p = lax.rem(me2[q] + d, n2[q])
        return rcopy(t_b.at[q], g1.at[q, me2[q]], sem_g1.at[0, q, d], sem_g1.at[1, q, d], dev2[q](p))

    def start_g1(d):
        for q in range(2):
            copy_g1(q, d).start()
    each(NY, start_g1)
    for q in range(2):
        g1[q, me2[q]] = t_b[q]

    def wait_g1(d):
        for q in range(2):
            copy_g1(q, d).wait_recv()
    each(NY, wait_g1)

    def copy_g2(q, d):
        p = lax.rem(me1[q] + d, n1[q])
        return rcopy(g1.at[q], g2.at[core * 2 + q, me1[q]], sem_g2.at[0, q, d], sem_g2.at[1, q, d], dev1[q](p))

    def start_g2(d):
        for q in range(2):
            copy_g2(q, d).start()
    each(NY, start_g2)
    for q in range(2):
        g2[core * 2 + q, me1[q]] = g1[q]

    def wait_g2(d):
        for q in range(2):
            copy_g2(q, d).wait_recv()
    each(NY, wait_g2)
    mine = g2.at[pl.ds(2 * core, 2)]
    last_copy = rcopy(mine, mine, sem_gc.at[0], sem_gc.at[1], other_core)
    last_copy.start()
    last_copy.wait_recv()

    for q in range(4):
        flat = g2[q].reshape(1024, 128)
        for t in range(9):
            gw_ref[t // 3, t % 3, :, q * 128:(q + 1) * 128] = flat[t * OP:t * OP + CO]
        if q == 0:
            tail = flat[9 * OP:9 * OP + 16].astype(F32)
            gb_ref[...] = (tail[0:1] + tail[1:2] + tail[2:3])[:, :CO]

    h_first.wait_send()
    h_last.wait_send()

    @pl.when(up)
    def _():
        row_up.wait_send()
        g_up.wait_send()
        for s in range(2):
            c_copy(2, s).wait_send()

    @pl.when(down)
    def _():
        row_dn.wait_send()
        g_dn.wait_send()
        for s in range(2):
            c_copy(0, s).wait_send()
    for s in range(2):
        c_copy(1, s).wait_send()

    def finish(d):
        f_copy(d).wait_send()
        g_copy(d).wait_send()
        sc_copy(d).wait_send()
        for q in range(2):
            copy1(q, d).wait_send()
            copy2(q, d).wait_send()
            copy_g1(q, d).wait_send()
            copy_g2(q, d).wait_send()
    each(NM, finish)
    each(NX, lambda d: copy3(d).wait_send())
    core_copy.wait_send()
    last_copy.wait_send()


def solution(mesh):
    NM, NLAT, NLON = (mesh.shape[k] for k in ("member", "lat", "lon"))
    NY, NX = NLAT // 2, NLON // 2 * 2
    sizes = (NM, NLAT, NLON, NY, NX)

    def on_device(inputs, weight, bias, observed, channel_weight):
        _, C, R, L = inputs.shape
        CO = weight.shape[2]
        rows = NLAT * R
        mean = 1.0 / (rows * math.sin(math.pi / (2 * rows)))
        every = jnp.asarray([math.sin(math.pi * (r + 0.5) / rows) / mean for r in range(rows)], F32)
        area = jnp.broadcast_to(every[:, None], (rows, 128))
        pad = ((0, 0), (0, 128 - CO))
        vm = pl.BlockSpec(memory_space=pltpu.VMEM)
        dma = pltpu.SemaphoreType.DMA
        V = pltpu.VMEM
        scratch = [
            V((C * R, 128), F32),
            V((C, R * 128), BF16),
            V((9 * OP, C), BF16),
            V((C, 1024), BF16),
            V((9 * OP, R * 128), F32),
            V((2, 16, C), BF16),
            V((2, 16, C), BF16),
            V((2, OF, 128), F32),
            V((2, OF, 128), F32),
            V((R, OP, 128), BF16),
            V((NM, OP, 128), BF16),
            V((OF * R, 128), F32),
            V((NM, OP, 128), BF16),
            V((R, OP, 128), BF16),
            V((OP, 128), BF16),
            V((R, OP, 128), BF16),
            V((2, 16, 128), BF16),
            V((3, 2, 16, 128), BF16),
            V((2, OP, 128), BF16),
            V((1024, R * 128), BF16),
            V((4, 1024, 128), F32),
            V((2, 1024, 128), F32),
            V((2, 1024, 128), F32),
            V((2, NY, 128, 128), F32),
            V((2, 128, 128), F32),
            V((2, NY, 16, 128), F32),
            V((NX, 2, 16, 128), F32),
            V((2, 16, 128), BF16),
            V((2, NY, 16, 128), BF16),
            V((4, NY, NY, 16, 128), BF16),
            V((C * R, 128), F32),
            dma((4,)), dma((4,)), dma((2, NM)), dma((2, NM)), dma((2, NM)), dma((4,)), dma((2, 3, 2)),
            dma((2,)), dma((2, 2, NY)), dma((2, 2, NY)), dma((2, NX)), dma((2, 2, NY)), dma((2, 2, NY)), dma((2,)),
        ]
        gi, gw, gb, score = pl.pallas_call(
            functools.partial(kernel, sizes),
            out_shape=(
                jax.ShapeDtypeStruct((C, R, L), BF16),
                jax.ShapeDtypeStruct((3, 3, CO, C), BF16),
                jax.ShapeDtypeStruct((1, CO), F32),
                jax.ShapeDtypeStruct((CO, R, L), BF16),
            ),
            in_specs=[vm] * 6,
            out_specs=(vm,) * 4,
            scratch_shapes=scratch,
            compiler_params=pltpu.CompilerParams(
                collective_id=0, has_side_effects=True, vmem_limit_bytes=56 * 1024 * 1024),
        )(inputs[0], weight, jnp.pad(bias[None], pad), observed, jnp.pad(channel_weight[None], pad), area)
        return gi[None], gw, gb[0], score

    in_specs = (P("member", None, "lat", "lon"), P(), P(), P(None, "lat", "lon"), P())
    out_specs = (P("member", None, "lat", "lon"), P(), P(), P(None, "lat", "lon"))
    return jax.shard_map(
        on_device, mesh=mesh, in_specs=in_specs, out_specs=out_specs, check_vma=False
    )
```

```python
import functools
import math

import jax
import jax.numpy as jnp
from jax import lax
from jax.experimental import pallas as pl
from jax.experimental.pallas import tpu as pltpu
from jax.sharding import PartitionSpec as P

smooth = 0.0625
MESH = pl.DeviceIdType.MESH
F32 = jnp.float32
BF16 = jnp.bfloat16
NN = (((1,), (0,)), ((), ()))
NT = (((1,), (1,)), ((), ()))
OP = 112
OF = 104


def mm(a, b, dims=NN):
    return lax.dot_general(a, b, dims, preferred_element_type=F32)


def rcopy(src, dst, ssem, rsem, dev):
    return pltpu.make_async_remote_copy(
        src_ref=src, dst_ref=dst, send_sem=ssem, recv_sem=rsem,
        device_id=dev, device_id_type=MESH,
    )


def kernel(
    sizes,
    x_in, w_in, bias_in, obs_in, cw_in,
    gi_ref, gw_ref, gb_ref, score_ref,
    x_ref, w_ref, bias_ref, obs_ref, cw_ref, sem_in,
    xf, xs, ws, wt, y, acc, yh, hs, hr, rows_s, rows_r, scale_s, fs, fr, of, gs, gr, sc_s, sc_r,
    ce_s, ce_r, rh, gt, d4, rc, rsum, r1, s3, t_b, g2, gif,
    sem_h, sem_row, sem_f, sem_g, sem_sc, sem_rh, sem_ce,
    sem_core, sem_1, sem_2, sem_g1, sem_gc, sem_here,
):
    NM, NLAT, NLON, NY, NX = sizes
    C = x_in.shape[0]
    CO = obs_in.shape[0]
    R = x_in.shape[1]
    m = lax.axis_index("member")
    a = lax.axis_index("lat")
    b = lax.axis_index("lon")
    xl, yy = a // NY, a % NY
    xh, core = b // 2, b % 2
    xx = xh * 2 + xl
    up = a > 0
    down = a < NLAT - 1
    left = lax.rem(b + NLON - 1, NLON)
    right = lax.rem(b + 1, NLON)
    a_up = jnp.maximum(a - 1, 0)
    a_dn = jnp.minimum(a + 1, NLAT - 1)

    def dev_z(p):
        return (p, a, b)

    def dev_y(p):
        return (m, xl * NY + p, b)

    def dev_x(p):
        return (m, (p % 2) * NY + yy, (p // 2) * 2 + core)

    other_core = (m, a, xh * 2 + 1 - core)

    def each(n, fn):
        def body(d, carry):
            fn(d)
            return carry
        lax.fori_loop(1, n, body, 0)

    pairs = ((x_in, x_ref), (w_in, w_ref), (bias_in, bias_ref), (cw_in, cw_ref), (obs_in, obs_ref))
    loads = [pltpu.make_async_copy(src, dst, sem_in.at[i]) for i, (src, dst) in enumerate(pairs)]
    for load in loads:
        load.start()
    sends = []
    late = []

    bar = pltpu.get_barrier_semaphore()

    def greet(dev):
        pl.semaphore_signal(bar, inc=1, device_id=dev, device_id_type=MESH)

    def peer(g, e, back=False):
        sign = -1 if back else 1
        p = (xx + NX + sign * (e // 8)) % NX
        step = NY + sign * (e % 8)
        y2 = (yy + step) % NY if g == 0 else yy
        m2 = (m + step) % NM if g == 1 else m
        return p, y2, m2

    def dev_of(p, y2, m2):
        return (m2, (p % 2) * NY + y2, (p // 2) * 2 + core)

    each(NM, lambda d: greet(dev_z(lax.rem(m + d, NM))))
    each(NY, lambda d: greet(dev_y(lax.rem(yy + d, NY))))
    each(NX, lambda d: greet(dev_x(lax.rem(xx + d, NX))))
    for bb in (left, right):
        greet((m, a, bb))

    @pl.when(up)
    def _():
        for bb in (b, left, right):
            greet((m, a_up, bb))

    @pl.when(down)
    def _():
        for bb in (b, left, right):
            greet((m, a_dn, bb))
    greet(other_core)

    loads[0].wait()
    xf[...] = x_ref[...].reshape(C * R, 128).astype(F32)
    for r in range(R):
        xs[:, r * 128:(r + 1) * 128] = xf[pl.ds(r, C, stride=R), :].astype(BF16)
    cell = lax.broadcasted_iota(jnp.int32, (32, R * 128), 1)
    line = lax.broadcasted_iota(jnp.int32, (32, R * 128), 0)
    want = jnp.where(line < 16, line * 128, (line - 16) * 128 + 127)
    pick = jnp.where((cell == want) & (line % 16 < R), 1.0, 0.0).astype(BF16)
    hs[...] = mm(pick, xs[...], NT).astype(BF16).reshape(2, 16, C)

    for load in loads[1:]:
        load.wait()
    zpad = jnp.zeros((OP - CO, C), F32)
    for t in range(9):
        tap = w_ref[t // 3, t % 3].astype(F32)
        ws[t * OP:(t + 1) * OP, :] = jnp.concatenate([tap, zpad], axis=0).astype(BF16)


    lane = lax.broadcasted_iota(jnp.int32, (OF, 128), 1)

    def shifted(p0, p1, p2):
        low = jnp.where(lane == 0, 0.0, pltpu.roll(p0, 1, 1))
        high = jnp.where(lane == 127, 0.0, pltpu.roll(p2, 127, 1))
        return p1 + low + high

    rows_s[0] = shifted(*[mm(ws[(6 + j) * OP:(6 + j) * OP + OF, :], xs[:, :128]) for j in range(3)])
    rows_s[1] = shifted(*[mm(ws[j * OP:j * OP + OF, :], xs[:, (R - 1) * 128:]) for j in range(3)])
    n_hello = (NM - 1) + (NY - 1) + (NX - 1) + 3
    pl.semaphore_wait(bar, n_hello + 3 * up.astype(jnp.int32) + 3 * down.astype(jnp.int32))
    each(NX, lambda d: pl.semaphore_signal(
        sem_here, inc=1, device_id=dev_x(lax.rem(xx + d, NX)), device_id_type=MESH))

    x_up = rcopy(rows_s.at[0], rows_r.at[1], sem_row.at[0], sem_row.at[3], (m, a_up, b))
    x_dn = rcopy(rows_s.at[1], rows_r.at[0], sem_row.at[1], sem_row.at[2], (m, a_dn, b))

    def h_copy(v, s):
        aa = (a_dn, a, a_up)[v]
        bb = right if s == 0 else left
        return rcopy(hs.at[1 - s], hr.at[v, s], sem_h.at[0, v, s], sem_h.at[1, v, s], (m, aa, bb))

    def both(fn):
        for s in range(2):
            fn(s)

    both(lambda s: h_copy(1, s).start())

    @pl.when(up)
    def _():
        both(lambda s: h_copy(2, s).start())
        x_up.start()

    @pl.when(down)
    def _():
        both(lambda s: h_copy(0, s).start())
        x_dn.start()

    def x_sent():
        both(lambda s: h_copy(1, s).wait_send())

        @pl.when(up)
        def _():
            x_up.wait_send()
            both(lambda s: h_copy(2, s).wait_send())

        @pl.when(down)
        def _():
            x_dn.wait_send()
            both(lambda s: h_copy(0, s).wait_send())
    sends.append(x_sent)

    for n in range(R // 2):
        at = slice(n * 256, (n + 1) * 256)
        y[:, at] = mm(ws[...], xs[:, at])
    fill = jnp.zeros((1, 128 - CO), F32)
    bt = jnp.broadcast_to(jnp.concatenate([bias_ref[...], fill], axis=1), (128, 128)).T
    ct = jnp.broadcast_to(jnp.concatenate([cw_ref[...], fill], axis=1), (128, 128)).T
    rows = NLAT * R
    row_at = jnp.full((8, 128), (a * R + m).astype(F32))
    area = jnp.cos(math.pi * (row_at + 0.5) / rows - math.pi / 2)
    area_mean = 1.0 / (rows * math.sin(math.pi / (2 * rows)))
    scale_s[...] = ct[:OP] * (area * (1.0 / area_mean))[0:1]

    def tap_rows(t):
        return slice(t * OP, t * OP + OF)

    for r in range(R):
        parts = []
        for j in range(3):
            total = None
            for i in range(3):
                src = r + i - 1
                if 0 <= src < R:
                    piece = y[tap_rows(i * 3 + j), src * 128:(src + 1) * 128]
                    total = piece if total is None else total + piece
            parts.append(total)
        acc[r] = shifted(*parts) + bt[:OF]

    both(lambda s: h_copy(1, s).wait_recv())

    @pl.when(up)
    def _():
        both(lambda s: h_copy(0, s).wait_recv())

    @pl.when(jnp.logical_not(up))
    def _():
        hr[0] = jnp.zeros((2, 16, C), BF16)

    @pl.when(down)
    def _():
        both(lambda s: h_copy(2, s).wait_recv())

    @pl.when(jnp.logical_not(down))
    def _():
        hr[2] = jnp.zeros((2, 16, C), BF16)
    yh[...] = mm(ws[...], hr[...].reshape(96, C), NT)

    pad8 = jnp.zeros((OP - OF, 128), F32)

    def pad16(v):
        return jnp.concatenate([v, pad8], axis=0).astype(BF16)

    def columns(r):
        cols = []
        for j in (0, 2):
            col = None
            for i in range(3):
                src = r + i - 1
                at = 8 * j + (R - 1 if src < 0 else 64 if src >= R else 32 + src)
                edge = yh[tap_rows(i * 3 + j), at:at + 1]
                col = edge if col is None else col + edge
            cols.append(col)
        return jnp.where(lane == 0, cols[0], jnp.where(lane == 127, cols[1], 0.0))

    def f_copy(d):
        p = lax.rem(m + d, NM)
        return rcopy(fs.at[p], fr.at[m], sem_f.at[0, d], sem_f.at[1, d], dev_z(p))

    def make_row(r):
        total = acc[r] + columns(r)
        if r == 0:
            total = total + rows_r[0]
        if r == R - 1:
            total = total + rows_r[1]
        fs[r] = pad16(total)

        @pl.when(m != r)
        def _():
            f_copy(lax.rem(r - m + NM, NM)).start()

    for r in range(1, R - 1):
        make_row(r)

    @pl.when(up)
    def _():
        x_dn.wait_recv()

    @pl.when(jnp.logical_not(up))
    def _():
        rows_r[0] = jnp.zeros((OF, 128), F32)

    @pl.when(down)
    def _():
        x_up.wait_recv()

    @pl.when(jnp.logical_not(down))
    def _():
        rows_r[1] = jnp.zeros((OF, 128), F32)
    make_row(0)
    make_row(R - 1)
    fr[m] = fs[m]
    sends.append(lambda: each(NM, lambda d: f_copy(d).wait_send()))
    of[...] = jnp.concatenate(
        [obs_ref[...].reshape(CO * R, 128).astype(F32), jnp.zeros(((OP - CO) * R, 128), F32)], axis=0)
    wt[:, :9 * OP] = ws[...].T
    wt[:, 9 * OP:] = jnp.zeros((C, 1024 - 9 * OP), BF16)
    each(NM, lambda d: f_copy(d).wait_recv())

    def score(c, carry):
        at = pl.ds(pl.multiple_of(c * 16, 16), 16)
        obs = of[pl.ds(c * (16 * R) + m, 16, stride=R), :]
        own = [fr[k, at, :].astype(F32) for k in range(NM)]
        slope = [None] * NM
        pair = jnp.full((16, 128), NM * 0.5 * math.sqrt(smooth), F32)
        gap_total = jnp.zeros((16, 128), F32)
        for k in range(NM):
            for n in range(k + 1, NM):
                diff = own[k] - own[n]
                sq = diff * diff + smooth
                inv = lax.rsqrt(sq)
                pair = pair + sq * inv
                s = diff * inv
                slope[k] = s if slope[k] is None else slope[k] + s
                slope[n] = -s if slope[n] is None else slope[n] - s
        for k in range(NM):
            gap = own[k] - obs
            sq = gap * gap + smooth
            inv = lax.rsqrt(sq)
            gap_total = gap_total + sq * inv
            gs[k, at, :] = (scale_s[at, :] * (
                gap * inv * (1.0 / NM) - slope[k] * (1.0 / (NM * (NM - 1))))).astype(BF16)
        sc_s[at, :] = (gap_total * (1.0 / NM) - pair * (1.0 / (NM * (NM - 1)))).astype(BF16)
        return carry
    lax.fori_loop(0, OP // 16, score, 0)

    def g_copy(d):
        p = lax.rem(m + d, NM)
        return rcopy(gs.at[p], gr.at[m], sem_g.at[0, d], sem_g.at[1, d], dev_z(p))

    def sc_copy(d):
        p = lax.rem(m + d, NM)
        return rcopy(sc_s, sc_r.at[m], sem_sc.at[0, d], sem_sc.at[1, d], dev_z(p))
    each(NM, lambda d: g_copy(d).start())
    gr[m] = gs[m]
    sends.append(lambda: each(NM, lambda d: g_copy(d).wait_send()))
    sc_r[m] = sc_s[...]
    each(NM, lambda d: g_copy(d).wait_recv())

    g_up = rcopy(gr.at[0], rh.at[1], sem_rh.at[0], sem_rh.at[3], (m, a_up, b))
    g_dn = rcopy(gr.at[R - 1], rh.at[0], sem_rh.at[1], sem_rh.at[2], (m, a_dn, b))

    @pl.when(up)
    def _():
        g_up.start()

    @pl.when(down)
    def _():
        g_dn.start()
    edges = []
    lane8 = lax.broadcasted_iota(jnp.int32, (8, 128), 1)
    line8 = lax.broadcasted_iota(jnp.int32, (8, 128), 0)
    pick2 = jnp.where(((line8 == 0) & (lane8 == 0)) | ((line8 == 1) & (lane8 == 127)), 1.0, 0.0).astype(BF16)
    for r in range(R):
        edges.append(mm(pick2, gr[r], NT))
    fill = jnp.zeros((16 - R, OP), F32)
    for side in range(2):
        stack = jnp.concatenate([e[side:side + 1] for e in edges] + [fill], axis=0)
        ce_s[side] = jnp.concatenate([stack, jnp.zeros((16, 128 - OP), F32)], axis=1).astype(BF16)

    def c_copy(v, s):
        aa = (a_dn, a, a_up)[v]
        bb = right if s == 0 else left
        return rcopy(ce_s.at[1 - s], ce_r.at[v, s], sem_ce.at[0, v, s], sem_ce.at[1, v, s], (m, aa, bb))

    for s in range(2):
        c_copy(1, s).start()

    @pl.when(down)
    def _():
        for s in range(2):
            c_copy(0, s).start()

    @pl.when(up)
    def _():
        for s in range(2):
            c_copy(2, s).start()

    def edges_sent():
        for s in range(2):
            c_copy(1, s).wait_send()

        @pl.when(up)
        def _():
            g_up.wait_send()
            for s in range(2):
                c_copy(2, s).wait_send()

        @pl.when(down)
        def _():
            g_dn.wait_send()
            for s in range(2):
                c_copy(0, s).wait_send()
    sends.append(edges_sent)

    for s in range(2):
        c_copy(1, s).wait_recv()

    @pl.when(up)
    def _():
        g_dn.wait_recv()
        for s in range(2):
            c_copy(0, s).wait_recv()

    @pl.when(jnp.logical_not(up))
    def _():
        rh[0] = jnp.zeros((OP, 128), BF16)
        for s in range(2):
            ce_r[0, s] = jnp.zeros((16, 128), BF16)

    @pl.when(down)
    def _():
        g_up.wait_recv()
        for s in range(2):
            c_copy(2, s).wait_recv()

    @pl.when(jnp.logical_not(down))
    def _():
        rh[1] = jnp.zeros((OP, 128), BF16)
        for s in range(2):
            ce_r[2, s] = jnp.zeros((16, 128), BF16)

    colt = []
    for s in range(2):
        above = ce_r[0, s].astype(F32)[R - 1:R]
        here = ce_r[1, s].astype(F32)[:R]
        below = ce_r[2, s].astype(F32)[0:1]
        stack = jnp.concatenate([above, here, below, jnp.zeros((128 - R - 2, 128), F32)], axis=0)
        colt.append(stack.T)
    lane_p = lax.broadcasted_iota(jnp.int32, (OP, 128), 1)
    for q in range(R + 2):
        r = q - 1
        mid = rh[0] if r < 0 else rh[1] if r >= R else gr[r]
        wide = mid.astype(F32)
        to_right = jnp.where(lane_p == 127, colt[1][:OP, q:q + 1], pltpu.roll(wide, 127, 1)).astype(BF16)
        to_left = jnp.where(lane_p == 0, colt[0][:OP, q:q + 1], pltpu.roll(wide, 1, 1)).astype(BF16)
        for i in range(3):
            here = r - 1 + i
            if 0 <= here < R:
                for j, v in enumerate((to_right, mid, to_left)):
                    t = i * 3 + j
                    gt[t * OP:(t + 1) * OP, here * 128:(here + 1) * 128] = v
    gt[9 * OP:, :] = jnp.zeros((1024 - 9 * OP, R * 128), BF16)

    half = C // 2

    def wgrad(h):
        at = pl.ds(pl.multiple_of(h * half, half), half)
        part = mm(gt[:9 * OP, :], xs[at, :], NT)
        for q in range(2):
            d4[h * 2 + q, :9 * OP, :] = part[:, q * 128:(q + 1) * 128]

    center = mm(jnp.ones((16, R * 128), BF16), gt[4 * OP:5 * OP, :], NT)
    bias_rows = jnp.concatenate([center, jnp.zeros((16, 128 - OP), F32)], axis=1)
    for q in range(4):
        d4[q, 9 * OP:, :] = bias_rows if q == 0 else jnp.zeros((16, 128), F32)
    wgrad(1 - core)
    core_copy = rcopy(d4.at[pl.ds(2 * (1 - core), 2)], rc, sem_core.at[0], sem_core.at[1], other_core)
    core_copy.start()
    sends.append(core_copy.wait_send)
    wgrad(core)
    core_copy.wait_recv()
    rsum[...] = d4[pl.ds(2 * core, 2)] + rc[...]

    own_chunk = (xx * NY + yy, xx * NM + m)

    def copy1(q, e):
        p, y2, m2 = peer(q, e)
        at = (p * 8 + (m2 if q else y2)) * 32
        return rcopy(rsum.at[q, pl.ds(pl.multiple_of(at, 32), 32)], r1.at[q, e],
                     sem_1.at[0, q, e], sem_1.at[1, q, e], dev_of(p, y2, m2))

    pl.semaphore_wait(sem_here, NX - 1)

    def start1(e):
        for q in range(2):
            copy1(q, e).start()
    each(32, start1)
    sends.append(lambda: each(32, lambda e: [copy1(q, e).wait_send() for q in range(2)]))
    each(NM, lambda d: sc_copy(d).start())
    sends.append(lambda: each(NM, lambda d: sc_copy(d).wait_send()))
    late.append(lambda: each(NM, lambda d: sc_copy(d).wait_recv()))

    def bwd(n, carry):
        at = pl.ds(pl.multiple_of(n * 256, 256), 256)
        part = mm(wt[...], gt[:, at])
        for q in range(2):
            gif[pl.ds(2 * n + q, C, stride=R), :] = part[:, q * 128:(q + 1) * 128]
        return carry
    lax.fori_loop(0, R // 2, bwd, 0)
    gi_ref[...] = gif[...].reshape(C, R, 128).astype(BF16)
    me2 = (m, yy)
    for q in range(2):
        def add(e, total):
            copy1(q, e).wait_recv()
            return total + r1[q, e]
        s3[q, me2[q]] = lax.fori_loop(
            1, 32, add, rsum[q, pl.ds(pl.multiple_of(own_chunk[q] * 32, 32), 32), :])

    def copy2(q, d):
        p = lax.rem(me2[q] + d, 8)
        mine = s3.at[q, me2[q]]
        return rcopy(mine, mine, sem_2.at[0, q, d], sem_2.at[1, q, d], dev_y(p) if q else dev_z(p))

    def start2(d):
        for q in range(2):
            copy2(q, d).start()
    each(8, start2)
    sends.append(lambda: each(8, lambda d: [copy2(q, d).wait_send() for q in range(2)]))

    def wait2(d):
        for q in range(2):
            copy2(q, d).wait_recv()
    each(8, wait2)
    factor = 1.0 / math.sqrt(NM * NLAT * R * NLON * 128)
    sub = lax.broadcasted_iota(jnp.int32, (32, 128), 0)
    for q in range(2):
        total = s3[q, 0]
        for p in range(1, 8):
            total = total + s3[q, p]
        total = total * factor
        high = total.astype(BF16).astype(F32)
        rest = total - high
        middle = rest.astype(BF16).astype(F32)
        low = rest - middle
        row = own_chunk[q] * 32 + sub
        t_b[q] = jnp.where(row == 9 * OP + 1, middle, jnp.where(row == 9 * OP + 2, low, high)).astype(BF16)

    def copy_g(q, e):
        return rcopy(t_b.at[q], g2.at[core * 2 + q, own_chunk[q]], sem_g1.at[0, q, e], sem_g1.at[1, q, e],
                     dev_of(*peer(q, e)))

    def start_g(e):
        for q in range(2):
            copy_g(q, e).start()
    each(32, start_g)
    sends.append(lambda: each(32, lambda e: [copy_g(q, e).wait_send() for q in range(2)]))
    for q in range(2):
        g2[core * 2 + q, own_chunk[q]] = t_b[q]

    def copy_c(q, k):
        at = pl.ds(pl.multiple_of(((xx + NX - k) % NX) * 8, 8), 8)
        block = g2.at[core * 2 + q, at]
        return rcopy(block, block, sem_gc.at[0, q, k], sem_gc.at[1, q, k], other_core)

    def pass_on(k, carry):
        def got(d, inner):
            for q in range(2):
                @pl.when(k + d > 0)
                def _():
                    copy_g(q, k * 8 + d).wait_recv()
            return inner
        lax.fori_loop(0, 8, got, 0)
        for q in range(2):
            copy_c(q, k).start()
        return carry
    lax.fori_loop(0, NX, pass_on, 0)

    def each_c(fn):
        def body(k, carry):
            for q in range(2):
                fn(copy_c(q, k))
            return carry
        lax.fori_loop(0, NX, body, 0)
    sends.append(lambda: each_c(lambda c: c.wait_send()))
    late.pop()()
    for r in range(R):
        of[pl.ds(r, OF, stride=R), :] = sc_r[r].astype(F32)[:OF]
    score_ref[...] = of[:CO * R, :].reshape(CO, R, 128).astype(BF16)

    each_c(lambda c: c.wait_recv())

    for q in range(4):
        flat = g2[q].reshape(1024, 128)
        for t in range(9):
            gw_ref[t // 3, t % 3, :, q * 128:(q + 1) * 128] = flat[t * OP:t * OP + CO]
        if q == 0:
            tail = flat[9 * OP:9 * OP + 16].astype(F32)
            gb_ref[...] = (tail[0:1] + tail[1:2] + tail[2:3])[:, :CO]

    for done in late + sends:
        done()


def write_out(*refs):
    loads, stores = [], []
    for k, cuts in enumerate((4, 3, 1, 1)):
        size = refs[k].shape[0] // cuts
        for c in range(cuts):
            at = pl.ds(c * size, size)
            n = len(loads)
            loads.append(pltpu.make_async_copy(refs[k].at[at], refs[8 + k].at[at], refs[12].at[0, n]))
            stores.append(pltpu.make_async_copy(refs[8 + k].at[at], refs[4 + k].at[at], refs[12].at[1, n]))
    for load in loads:
        load.start()
    for load, store in zip(loads, stores):
        load.wait()
        store.start()
    for store in stores:
        store.wait()


def solution(mesh):
    NM, NLAT, NLON = (mesh.shape[k] for k in ("member", "lat", "lon"))
    NY, NX = NLAT // 2, NLON // 2 * 2
    sizes = (NM, NLAT, NLON, NY, NX)

    def on_device(inputs, weight, bias, observed, channel_weight):
        _, C, R, L = inputs.shape
        CO = weight.shape[2]
        vm = pl.BlockSpec(memory_space=pltpu.VMEM)
        hbm = pl.BlockSpec(memory_space=pltpu.HBM)
        dma = pltpu.SemaphoreType.DMA
        V = pltpu.VMEM
        scratch = [
            V((C, R, 128), BF16), V((3, 3, CO, C), BF16), V((1, CO), F32), V((CO, R, 128), BF16), V((1, CO), F32), dma((5,)),
            V((C * R, 128), F32),
            V((C, R * 128), BF16),
            V((9 * OP, C), BF16),
            V((C, 1024), BF16),
            V((9 * OP, R * 128), F32),
            V((R, OF, 128), F32),
            V((9 * OP, 96), F32),
            V((2, 16, C), BF16),
            V((3, 2, 16, C), BF16),
            V((2, OF, 128), F32),
            V((2, OF, 128), F32),
            V((OP, 128), F32),
            V((R, OP, 128), BF16),
            V((NM, OP, 128), BF16),
            V((OP * R, 128), F32),
            V((NM, OP, 128), BF16),
            V((R, OP, 128), BF16),
            V((OP, 128), BF16),
            V((R, OP, 128), BF16),
            V((2, 16, 128), BF16),
            V((3, 2, 16, 128), BF16),
            V((2, OP, 128), BF16),
            V((1024, R * 128), BF16),
            V((4, 1024, 128), F32),
            V((2, 1024, 128), F32),
            V((2, 1024, 128), F32),
            V((2, 32, 32, 128), F32),
            V((2, 8, 32, 128), F32),
            V((2, 32, 128), BF16),
            V((4, 32, 32, 128), BF16),
            V((C * R, 128), F32),
            dma((2, 3, 2)), dma((4,)), dma((2, NM)), dma((2, NM)), dma((2, NM)), dma((4,)), dma((2, 3, 2)),
            dma((2,)), dma((2, 2, 32)), dma((2, 2, 8)), dma((2, 2, 32)), dma((2, 2, NX)),
            pltpu.SemaphoreType.REGULAR,
        ]
        shapes = (
            jax.ShapeDtypeStruct((C, R, L), BF16),
            jax.ShapeDtypeStruct((3, 3, CO, C), BF16),
            jax.ShapeDtypeStruct((1, CO), F32),
            jax.ShapeDtypeStruct((CO, R, L), BF16),
        )
        results = pl.pallas_call(
            functools.partial(kernel, sizes),
            out_shape=shapes,
            in_specs=[hbm] * 5,
            out_specs=(vm,) * 4,
            scratch_shapes=scratch,
            compiler_params=pltpu.CompilerParams(
                collective_id=0, has_side_effects=True, vmem_limit_bytes=58 * 1024 * 1024),
        )(inputs[0], weight, bias[None], observed, channel_weight[None])
        gi, gw, gb, score = pl.pallas_call(
            write_out,
            out_shape=shapes,
            in_specs=[hbm] * 4,
            out_specs=(hbm,) * 4,
            scratch_shapes=[V(shape.shape, shape.dtype) for shape in shapes] + [dma((2, 9))],
            compiler_params=pltpu.CompilerParams(vmem_limit_bytes=58 * 1024 * 1024),
        )(*results)
        return gi[None], gw, gb[0], score

    in_specs = (P("member", None, "lat", "lon"), P(), P(), P(None, "lat", "lon"), P())
    out_specs = (P("member", None, "lat", "lon"), P(), P(), P(None, "lat", "lon"))
    return jax.shard_map(
        on_device, mesh=mesh, in_specs=in_specs, out_specs=out_specs, check_vma=False
    )
```

```python
import functools
import math

import jax
import jax.numpy as jnp
from jax import lax
from jax.experimental import pallas as pl
from jax.experimental.pallas import tpu as pltpu
from jax.sharding import PartitionSpec as P

smooth = 0.0625
MESH = pl.DeviceIdType.MESH
F32 = jnp.float32
BF16 = jnp.bfloat16
NN = (((1,), (0,)), ((), ()))
NT = (((1,), (1,)), ((), ()))
OP = 112
OF = 104


def mm(a, b, dims=NN):
    return lax.dot_general(a, b, dims, preferred_element_type=F32)


def rcopy(src, dst, ssem, rsem, dev):
    return pltpu.make_async_remote_copy(
        src_ref=src, dst_ref=dst, send_sem=ssem, recv_sem=rsem,
        device_id=dev, device_id_type=MESH,
    )


def kernel(
    sizes,
    x_in, w_in, bias_in, obs_in, cw_in,
    gi_ref, gw_ref, gb_ref, score_ref,
    x_ref, w_ref, bias_ref, obs_ref, cw_ref, sem_in,
    xf, xs, ws, wt, y, acc, yh, hs, hr, rows_s, rows_r, scale_s, fs, fr, of, gs, gr, sc_s, sc_r,
    ce_s, ce_r, rh, gt, d4, rc, rsum, r1, s3, t_b, g2, gif,
    sem_h, sem_row, sem_f, sem_g, sem_sc, sem_rh, sem_ce,
    sem_core, sem_1, sem_2, sem_g1, sem_gc, sem_here,
):
    NM, NLAT, NLON, NY, NX = sizes
    C = x_in.shape[0]
    CO = obs_in.shape[0]
    R = x_in.shape[1]
    m = lax.axis_index("member")
    a = lax.axis_index("lat")
    b = lax.axis_index("lon")
    xl, yy = a // NY, a % NY
    xh, core = b // 2, b % 2
    xx = xh * 2 + xl
    up = a > 0
    down = a < NLAT - 1
    left = lax.rem(b + NLON - 1, NLON)
    right = lax.rem(b + 1, NLON)
    a_up = jnp.maximum(a - 1, 0)
    a_dn = jnp.minimum(a + 1, NLAT - 1)

    def dev_z(p):
        return (p, a, b)

    def dev_y(p):
        return (m, xl * NY + p, b)

    def dev_x(p):
        return (m, (p % 2) * NY + yy, (p // 2) * 2 + core)

    other_core = (m, a, xh * 2 + 1 - core)

    def each(n, fn):
        def body(d, carry):
            fn(d)
            return carry
        lax.fori_loop(1, n, body, 0)

    pairs = ((x_in, x_ref), (w_in, w_ref), (bias_in, bias_ref), (cw_in, cw_ref), (obs_in, obs_ref))
    loads = [pltpu.make_async_copy(src, dst, sem_in.at[i]) for i, (src, dst) in enumerate(pairs)]
    for load in loads:
        load.start()
    sends = []
    late = []

    bar = pltpu.get_barrier_semaphore()

    def greet(dev):
        pl.semaphore_signal(bar, inc=1, device_id=dev, device_id_type=MESH)

    def peer(g, e, back=False):
        sign = -1 if back else 1
        p = (xx + NX + sign * (e // 8)) % NX
        step = NY + sign * (e % 8)
        y2 = (yy + step) % NY if g == 0 else yy
        m2 = (m + step) % NM if g == 1 else m
        return p, y2, m2

    def dev_of(p, y2, m2):
        return (m2, (p % 2) * NY + y2, (p // 2) * 2 + core)

    each(NM, lambda d: greet(dev_z(lax.rem(m + d, NM))))
    each(NY, lambda d: greet(dev_y(lax.rem(yy + d, NY))))
    each(NX, lambda d: greet(dev_x(lax.rem(xx + d, NX))))
    for bb in (left, right):
        greet((m, a, bb))

    @pl.when(up)
    def _():
        for bb in (b, left, right):
            greet((m, a_up, bb))

    @pl.when(down)
    def _():
        for bb in (b, left, right):
            greet((m, a_dn, bb))
    greet(other_core)

    loads[0].wait()
    xf[...] = x_ref[...].reshape(C * R, 128).astype(F32)
    for r in range(R):
        xs[:, r * 128:(r + 1) * 128] = xf[pl.ds(r, C, stride=R), :].astype(BF16)
    cell = lax.broadcasted_iota(jnp.int32, (32, R * 128), 1)
    line = lax.broadcasted_iota(jnp.int32, (32, R * 128), 0)
    want = jnp.where(line < 16, line * 128, (line - 16) * 128 + 127)
    pick = jnp.where((cell == want) & (line % 16 < R), 1.0, 0.0).astype(BF16)
    hs[...] = mm(pick, xs[...], NT).astype(BF16).reshape(2, 16, C)

    for load in loads[1:]:
        load.wait()
    zpad = jnp.zeros((OP - CO, C), F32)
    for t in range(9):
        tap = w_ref[t // 3, t % 3].astype(F32)
        ws[t * OP:(t + 1) * OP, :] = jnp.concatenate([tap, zpad], axis=0).astype(BF16)


    lane = lax.broadcasted_iota(jnp.int32, (OF, 128), 1)

    def shifted(p0, p1, p2):
        low = jnp.where(lane == 0, 0.0, pltpu.roll(p0, 1, 1))
        high = jnp.where(lane == 127, 0.0, pltpu.roll(p2, 127, 1))
        return p1 + low + high

    rows_s[0] = shifted(*[mm(ws[(6 + j) * OP:(6 + j) * OP + OF, :], xs[:, :128]) for j in range(3)])
    rows_s[1] = shifted(*[mm(ws[j * OP:j * OP + OF, :], xs[:, (R - 1) * 128:]) for j in range(3)])
    n_hello = (NM - 1) + (NY - 1) + (NX - 1) + 3
    pl.semaphore_wait(bar, n_hello + 3 * up.astype(jnp.int32) + 3 * down.astype(jnp.int32))
    each(NX, lambda d: pl.semaphore_signal(
        sem_here, inc=1, device_id=dev_x(lax.rem(xx + d, NX)), device_id_type=MESH))

    x_up = rcopy(rows_s.at[0], rows_r.at[1], sem_row.at[0], sem_row.at[3], (m, a_up, b))
    x_dn = rcopy(rows_s.at[1], rows_r.at[0], sem_row.at[1], sem_row.at[2], (m, a_dn, b))

    def h_copy(v, s):
        aa = (a_dn, a, a_up)[v]
        bb = right if s == 0 else left
        return rcopy(hs.at[1 - s], hr.at[v, s], sem_h.at[0, v, s], sem_h.at[1, v, s], (m, aa, bb))

    def both(fn):
        for s in range(2):
            fn(s)

    both(lambda s: h_copy(1, s).start())

    @pl.when(up)
    def _():
        both(lambda s: h_copy(2, s).start())
        x_up.start()

    @pl.when(down)
    def _():
        both(lambda s: h_copy(0, s).start())
        x_dn.start()

    def x_sent():
        both(lambda s: h_copy(1, s).wait_send())

        @pl.when(up)
        def _():
            x_up.wait_send()
            both(lambda s: h_copy(2, s).wait_send())

        @pl.when(down)
        def _():
            x_dn.wait_send()
            both(lambda s: h_copy(0, s).wait_send())
    sends.append(x_sent)

    for n in range(R // 2):
        at = slice(n * 256, (n + 1) * 256)
        y[:, at] = mm(ws[...], xs[:, at])
    fill = jnp.zeros((1, 128 - CO), F32)
    bt = jnp.broadcast_to(jnp.concatenate([bias_ref[...], fill], axis=1), (128, 128)).T
    ct = jnp.broadcast_to(jnp.concatenate([cw_ref[...], fill], axis=1), (128, 128)).T
    rows = NLAT * R
    row_at = jnp.full((8, 128), (a * R + m).astype(F32))
    area = jnp.cos(math.pi * (row_at + 0.5) / rows - math.pi / 2)
    area_mean = 1.0 / (rows * math.sin(math.pi / (2 * rows)))
    scale_s[...] = ct[:OP] * (area * (1.0 / area_mean))[0:1]

    def tap_rows(t):
        return slice(t * OP, t * OP + OF)

    for r in range(R):
        parts = []
        for j in range(3):
            total = None
            for i in range(3):
                src = r + i - 1
                if 0 <= src < R:
                    piece = y[tap_rows(i * 3 + j), src * 128:(src + 1) * 128]
                    total = piece if total is None else total + piece
            parts.append(total)
        acc[r] = shifted(*parts) + bt[:OF]

    both(lambda s: h_copy(1, s).wait_recv())

    @pl.when(up)
    def _():
        both(lambda s: h_copy(0, s).wait_recv())

    @pl.when(jnp.logical_not(up))
    def _():
        hr[0] = jnp.zeros((2, 16, C), BF16)

    @pl.when(down)
    def _():
        both(lambda s: h_copy(2, s).wait_recv())

    @pl.when(jnp.logical_not(down))
    def _():
        hr[2] = jnp.zeros((2, 16, C), BF16)
    lines = []
    for s in range(2):
        lines += [hr[0, s].astype(F32)[R - 1:R], hr[1, s].astype(F32)[:R], hr[2, s].astype(F32)[0:1],
                  jnp.zeros((14 - R, C), F32)]
    lines.append(jnp.zeros((96, C), F32))
    yh[...] = mm(ws[...], jnp.concatenate(lines, axis=0).astype(BF16), NT)
    sides = []
    for j in (0, 2):
        sides.append(yh[tap_rows(j), :] + pltpu.roll(yh[tap_rows(3 + j), :], 127, 1)
                     + pltpu.roll(yh[tap_rows(6 + j), :], 126, 1))

    pad8 = jnp.zeros((OP - OF, 128), F32)

    def pad16(v):
        return jnp.concatenate([v, pad8], axis=0).astype(BF16)

    def columns(r):
        low = sides[0][:, r:r + 1]
        high = sides[1][:, 16 + r:17 + r]
        return jnp.where(lane == 0, low, jnp.where(lane == 127, high, 0.0))

    def f_copy(d):
        p = lax.rem(m + d, NM)
        return rcopy(fs.at[p], fr.at[m], sem_f.at[0, d], sem_f.at[1, d], dev_z(p))

    def make_row(r):
        total = acc[r] + columns(r)
        if r == 0:
            total = total + rows_r[0]
        if r == R - 1:
            total = total + rows_r[1]
        fs[r] = pad16(total)

        @pl.when(m != r)
        def _():
            f_copy(lax.rem(r - m + NM, NM)).start()

    for r in range(1, R - 1):
        make_row(r)

    @pl.when(up)
    def _():
        x_dn.wait_recv()

    @pl.when(jnp.logical_not(up))
    def _():
        rows_r[0] = jnp.zeros((OF, 128), F32)

    @pl.when(down)
    def _():
        x_up.wait_recv()

    @pl.when(jnp.logical_not(down))
    def _():
        rows_r[1] = jnp.zeros((OF, 128), F32)
    make_row(0)
    make_row(R - 1)
    fr[m] = fs[m]
    sends.append(lambda: each(NM, lambda d: f_copy(d).wait_send()))
    of[...] = jnp.concatenate(
        [obs_ref[...].reshape(CO * R, 128).astype(F32), jnp.zeros(((OP - CO) * R, 128), F32)], axis=0)
    wt[:, :9 * OP] = ws[...].T
    wt[:, 9 * OP:] = jnp.zeros((C, 1024 - 9 * OP), BF16)
    each(NM, lambda d: f_copy(d).wait_recv())

    def score(c, carry):
        at = pl.ds(pl.multiple_of(c * 16, 16), 16)
        obs = of[pl.ds(c * (16 * R) + m, 16, stride=R), :]
        own = [fr[k, at, :].astype(F32) for k in range(NM)]
        slope = [None] * NM
        pair = jnp.full((16, 128), NM * 0.5 * math.sqrt(smooth), F32)
        gap_total = jnp.zeros((16, 128), F32)
        for k in range(NM):
            for n in range(k + 1, NM):
                diff = own[k] - own[n]
                sq = diff * diff + smooth
                inv = lax.rsqrt(sq)
                pair = pair + sq * inv
                s = diff * inv
                slope[k] = s if slope[k] is None else slope[k] + s
                slope[n] = -s if slope[n] is None else slope[n] - s
        for k in range(NM):
            gap = own[k] - obs
            sq = gap * gap + smooth
            inv = lax.rsqrt(sq)
            gap_total = gap_total + sq * inv
            gs[k, at, :] = (scale_s[at, :] * (
                gap * inv * (1.0 / NM) - slope[k] * (1.0 / (NM * (NM - 1))))).astype(BF16)
        sc_s[at, :] = (gap_total * (1.0 / NM) - pair * (1.0 / (NM * (NM - 1)))).astype(BF16)
        return carry
    lax.fori_loop(0, OP // 16, score, 0)

    def g_copy(d):
        p = lax.rem(m + d, NM)
        return rcopy(gs.at[p], gr.at[m], sem_g.at[0, d], sem_g.at[1, d], dev_z(p))

    def sc_copy(d):
        p = lax.rem(m + d, NM)
        return rcopy(sc_s, sc_r.at[m], sem_sc.at[0, d], sem_sc.at[1, d], dev_z(p))
    each(NM, lambda d: g_copy(d).start())
    gr[m] = gs[m]
    sends.append(lambda: each(NM, lambda d: g_copy(d).wait_send()))
    sc_r[m] = sc_s[...]
    each(NM, lambda d: g_copy(d).wait_recv())

    g_up = rcopy(gr.at[0], rh.at[1], sem_rh.at[0], sem_rh.at[3], (m, a_up, b))
    g_dn = rcopy(gr.at[R - 1], rh.at[0], sem_rh.at[1], sem_rh.at[2], (m, a_dn, b))

    @pl.when(up)
    def _():
        g_up.start()

    @pl.when(down)
    def _():
        g_dn.start()
    edges = []
    lane8 = lax.broadcasted_iota(jnp.int32, (8, 128), 1)
    line8 = lax.broadcasted_iota(jnp.int32, (8, 128), 0)
    pick2 = jnp.where(((line8 == 0) & (lane8 == 0)) | ((line8 == 1) & (lane8 == 127)), 1.0, 0.0).astype(BF16)
    for r in range(R):
        edges.append(mm(pick2, gr[r], NT))
    fill = jnp.zeros((16 - R, OP), F32)
    for side in range(2):
        stack = jnp.concatenate([e[side:side + 1] for e in edges] + [fill], axis=0)
        ce_s[side] = jnp.concatenate([stack, jnp.zeros((16, 128 - OP), F32)], axis=1).astype(BF16)

    def c_copy(v, s):
        aa = (a_dn, a, a_up)[v]
        bb = right if s == 0 else left
        return rcopy(ce_s.at[1 - s], ce_r.at[v, s], sem_ce.at[0, v, s], sem_ce.at[1, v, s], (m, aa, bb))

    for s in range(2):
        c_copy(1, s).start()

    @pl.when(down)
    def _():
        for s in range(2):
            c_copy(0, s).start()

    @pl.when(up)
    def _():
        for s in range(2):
            c_copy(2, s).start()

    def edges_sent():
        for s in range(2):
            c_copy(1, s).wait_send()

        @pl.when(up)
        def _():
            g_up.wait_send()
            for s in range(2):
                c_copy(2, s).wait_send()

        @pl.when(down)
        def _():
            g_dn.wait_send()
            for s in range(2):
                c_copy(0, s).wait_send()
    sends.append(edges_sent)

    for s in range(2):
        c_copy(1, s).wait_recv()

    @pl.when(up)
    def _():
        g_dn.wait_recv()
        for s in range(2):
            c_copy(0, s).wait_recv()

    @pl.when(jnp.logical_not(up))
    def _():
        rh[0] = jnp.zeros((OP, 128), BF16)
        for s in range(2):
            ce_r[0, s] = jnp.zeros((16, 128), BF16)

    @pl.when(down)
    def _():
        g_up.wait_recv()
        for s in range(2):
            c_copy(2, s).wait_recv()

    @pl.when(jnp.logical_not(down))
    def _():
        rh[1] = jnp.zeros((OP, 128), BF16)
        for s in range(2):
            ce_r[2, s] = jnp.zeros((16, 128), BF16)

    colt = []
    for s in range(2):
        above = ce_r[0, s].astype(F32)[R - 1:R]
        here = ce_r[1, s].astype(F32)[:R]
        below = ce_r[2, s].astype(F32)[0:1]
        stack = jnp.concatenate([above, here, below, jnp.zeros((128 - R - 2, 128), F32)], axis=0)
        colt.append(stack.T)
    lane_p = lax.broadcasted_iota(jnp.int32, (OP, 128), 1)
    for q in range(R + 2):
        r = q - 1
        mid = rh[0] if r < 0 else rh[1] if r >= R else gr[r]
        wide = mid.astype(F32)
        to_right = jnp.where(lane_p == 127, colt[1][:OP, q:q + 1], pltpu.roll(wide, 127, 1)).astype(BF16)
        to_left = jnp.where(lane_p == 0, colt[0][:OP, q:q + 1], pltpu.roll(wide, 1, 1)).astype(BF16)
        for i in range(3):
            here = r - 1 + i
            if 0 <= here < R:
                for j, v in enumerate((to_right, mid, to_left)):
                    t = i * 3 + j
                    gt[t * OP:(t + 1) * OP, here * 128:(here + 1) * 128] = v
    gt[9 * OP:, :] = jnp.zeros((1024 - 9 * OP, R * 128), BF16)

    half = C // 2

    def wgrad(h):
        at = pl.ds(pl.multiple_of(h * half, half), half)
        part = mm(gt[:9 * OP, :], xs[at, :], NT)
        for q in range(2):
            d4[h * 2 + q, :9 * OP, :] = part[:, q * 128:(q + 1) * 128]

    center = mm(jnp.ones((16, R * 128), BF16), gt[4 * OP:5 * OP, :], NT)
    bias_rows = jnp.concatenate([center, jnp.zeros((16, 128 - OP), F32)], axis=1)
    for q in range(4):
        d4[q, 9 * OP:, :] = bias_rows if q == 0 else jnp.zeros((16, 128), F32)
    wgrad(1 - core)
    core_copy = rcopy(d4.at[pl.ds(2 * (1 - core), 2)], rc, sem_core.at[0], sem_core.at[1], other_core)
    core_copy.start()
    sends.append(core_copy.wait_send)
    wgrad(core)
    core_copy.wait_recv()
    rsum[...] = d4[pl.ds(2 * core, 2)] + rc[...]

    own_chunk = (xx * NY + yy, xx * NM + m)

    def copy1(q, e):
        p, y2, m2 = peer(q, e)
        at = (p * 8 + (m2 if q else y2)) * 32
        return rcopy(rsum.at[q, pl.ds(pl.multiple_of(at, 32), 32)], r1.at[q, e],
                     sem_1.at[0, q, e], sem_1.at[1, q, e], dev_of(p, y2, m2))

    pl.semaphore_wait(sem_here, NX - 1)

    def start1(e):
        for q in range(2):
            copy1(q, e).start()
    each(32, start1)
    sends.append(lambda: each(32, lambda e: [copy1(q, e).wait_send() for q in range(2)]))
    each(NM, lambda d: sc_copy(d).start())
    sends.append(lambda: each(NM, lambda d: sc_copy(d).wait_send()))
    late.append(lambda: each(NM, lambda d: sc_copy(d).wait_recv()))

    def bwd(n, carry):
        at = pl.ds(pl.multiple_of(n * 256, 256), 256)
        part = mm(wt[...], gt[:, at])
        for q in range(2):
            gif[pl.ds(2 * n + q, C, stride=R), :] = part[:, q * 128:(q + 1) * 128]
        return carry
    lax.fori_loop(0, R // 2, bwd, 0)
    gi_ref[...] = gif[...].reshape(C, R, 128).astype(BF16)
    me2 = (m, yy)
    for q in range(2):
        def add(e, total):
            copy1(q, e).wait_recv()
            return total + r1[q, e]
        s3[q, me2[q]] = lax.fori_loop(
            1, 32, add, rsum[q, pl.ds(pl.multiple_of(own_chunk[q] * 32, 32), 32), :])

    def copy2(q, d):
        p = lax.rem(me2[q] + d, 8)
        mine = s3.at[q, me2[q]]
        return rcopy(mine, mine, sem_2.at[0, q, d], sem_2.at[1, q, d], dev_y(p) if q else dev_z(p))

    def start2(d):
        for q in range(2):
            copy2(q, d).start()
    each(8, start2)
    sends.append(lambda: each(8, lambda d: [copy2(q, d).wait_send() for q in range(2)]))

    def wait2(d):
        for q in range(2):
            copy2(q, d).wait_recv()
    each(8, wait2)
    factor = 1.0 / math.sqrt(NM * NLAT * R * NLON * 128)
    sub = lax.broadcasted_iota(jnp.int32, (32, 128), 0)
    for q in range(2):
        total = s3[q, 0]
        for p in range(1, 8):
            total = total + s3[q, p]
        total = total * factor
        high = total.astype(BF16).astype(F32)
        rest = total - high
        middle = rest.astype(BF16).astype(F32)
        low = rest - middle
        row = own_chunk[q] * 32 + sub
        t_b[q] = jnp.where(row == 9 * OP + 1, middle, jnp.where(row == 9 * OP + 2, low, high)).astype(BF16)

    def copy_g(q, e):
        return rcopy(t_b.at[q], g2.at[core * 2 + q, own_chunk[q]], sem_g1.at[0, q, e], sem_g1.at[1, q, e],
                     dev_of(*peer(q, e)))

    def start_g(e):
        for q in range(2):
            copy_g(q, e).start()
    each(32, start_g)
    sends.append(lambda: each(32, lambda e: [copy_g(q, e).wait_send() for q in range(2)]))
    for q in range(2):
        g2[core * 2 + q, own_chunk[q]] = t_b[q]

    def copy_c(q, k):
        at = pl.ds(pl.multiple_of(((xx + NX - k) % NX) * 8, 8), 8)
        block = g2.at[core * 2 + q, at]
        return rcopy(block, block, sem_gc.at[0, q, k], sem_gc.at[1, q, k], other_core)

    def pass_on(k, carry):
        def got(d, inner):
            for q in range(2):
                @pl.when(k + d > 0)
                def _():
                    copy_g(q, k * 8 + d).wait_recv()
            return inner
        lax.fori_loop(0, 8, got, 0)
        for q in range(2):
            copy_c(q, k).start()
        return carry
    lax.fori_loop(0, NX, pass_on, 0)

    def each_c(fn):
        def body(k, carry):
            for q in range(2):
                fn(copy_c(q, k))
            return carry
        lax.fori_loop(0, NX, body, 0)
    sends.append(lambda: each_c(lambda c: c.wait_send()))
    late.pop()()
    for r in range(R):
        of[pl.ds(r, OF, stride=R), :] = sc_r[r].astype(F32)[:OF]
    score_ref[...] = of[:CO * R, :].reshape(CO, R, 128).astype(BF16)

    each_c(lambda c: c.wait_recv())

    for q in range(4):
        flat = g2[q].reshape(1024, 128)
        for t in range(9):
            gw_ref[t // 3, t % 3, :, q * 128:(q + 1) * 128] = flat[t * OP:t * OP + CO]
        if q == 0:
            tail = flat[9 * OP:9 * OP + 16].astype(F32)
            gb_ref[...] = (tail[0:1] + tail[1:2] + tail[2:3])[:, :CO]

    for done in late + sends:
        done()


def write_out(*refs):
    loads, stores = [], []
    for k, cuts in enumerate((8, 3, 1, 2)):
        size = refs[k].shape[0] // cuts
        for c in range(cuts):
            at = pl.ds(c * size, size)
            n = len(loads)
            loads.append(pltpu.make_async_copy(refs[k].at[at], refs[8 + k].at[at], refs[12].at[0, n]))
            stores.append(pltpu.make_async_copy(refs[8 + k].at[at], refs[4 + k].at[at], refs[12].at[1, n]))
    for load in loads:
        load.start()
    for load, store in zip(loads, stores):
        load.wait()
        store.start()
    for store in stores:
        store.wait()


def solution(mesh):
    NM, NLAT, NLON = (mesh.shape[k] for k in ("member", "lat", "lon"))
    NY, NX = NLAT // 2, NLON // 2 * 2
    sizes = (NM, NLAT, NLON, NY, NX)

    def on_device(inputs, weight, bias, observed, channel_weight):
        _, C, R, L = inputs.shape
        CO = weight.shape[2]
        vm = pl.BlockSpec(memory_space=pltpu.VMEM)
        hbm = pl.BlockSpec(memory_space=pltpu.HBM)
        dma = pltpu.SemaphoreType.DMA
        V = pltpu.VMEM
        scratch = [
            V((C, R, 128), BF16), V((3, 3, CO, C), BF16), V((1, CO), F32), V((CO, R, 128), BF16), V((1, CO), F32), dma((5,)),
            V((C * R, 128), F32),
            V((C, R * 128), BF16),
            V((9 * OP, C), BF16),
            V((C, 1024), BF16),
            V((9 * OP, R * 128), F32),
            V((R, OF, 128), F32),
            V((9 * OP, 128), F32),
            V((2, 16, C), BF16),
            V((3, 2, 16, C), BF16),
            V((2, OF, 128), F32),
            V((2, OF, 128), F32),
            V((OP, 128), F32),
            V((R, OP, 128), BF16),
            V((NM, OP, 128), BF16),
            V((OP * R, 128), F32),
            V((NM, OP, 128), BF16),
            V((R, OP, 128), BF16),
            V((OP, 128), BF16),
            V((R, OP, 128), BF16),
            V((2, 16, 128), BF16),
            V((3, 2, 16, 128), BF16),
            V((2, OP, 128), BF16),
            V((1024, R * 128), BF16),
            V((4, 1024, 128), F32),
            V((2, 1024, 128), F32),
            V((2, 1024, 128), F32),
            V((2, 32, 32, 128), F32),
            V((2, 8, 32, 128), F32),
            V((2, 32, 128), BF16),
            V((4, 32, 32, 128), BF16),
            V((C * R, 128), F32),
            dma((2, 3, 2)), dma((4,)), dma((2, NM)), dma((2, NM)), dma((2, NM)), dma((4,)), dma((2, 3, 2)),
            dma((2,)), dma((2, 2, 32)), dma((2, 2, 8)), dma((2, 2, 32)), dma((2, 2, NX)),
            pltpu.SemaphoreType.REGULAR,
        ]
        shapes = (
            jax.ShapeDtypeStruct((C, R, L), BF16),
            jax.ShapeDtypeStruct((3, 3, CO, C), BF16),
            jax.ShapeDtypeStruct((1, CO), F32),
            jax.ShapeDtypeStruct((CO, R, L), BF16),
        )
        results = pl.pallas_call(
            functools.partial(kernel, sizes),
            out_shape=shapes,
            in_specs=[hbm] * 5,
            out_specs=(vm,) * 4,
            scratch_shapes=scratch,
            compiler_params=pltpu.CompilerParams(
                collective_id=0, has_side_effects=True, vmem_limit_bytes=58 * 1024 * 1024),
        )(inputs[0], weight, bias[None], observed, channel_weight[None])
        gi, gw, gb, score = pl.pallas_call(
            write_out,
            out_shape=shapes,
            in_specs=[hbm] * 4,
            out_specs=(hbm,) * 4,
            scratch_shapes=[V(shape.shape, shape.dtype) for shape in shapes] + [dma((2, 14))],
            compiler_params=pltpu.CompilerParams(vmem_limit_bytes=58 * 1024 * 1024),
        )(*results)
        return gi[None], gw, gb[0], score

    in_specs = (P("member", None, "lat", "lon"), P(), P(), P(None, "lat", "lon"), P())
    out_specs = (P("member", None, "lat", "lon"), P(), P(), P(None, "lat", "lon"))
    return jax.shard_map(
        on_device, mesh=mesh, in_specs=in_specs, out_specs=out_specs, check_vma=False
    )
```
